256 devices in a mesh: dp: 32 (over x, y, z_lo), seq: 8 (over z_hi, core).
Axes of the slice: x: 4, y: 4, z: 8 (z_hi: 4, z_lo: 2; z = z_hi * 2 + z_lo), core: 2. Of those that a mesh axis runs over, the one named last changes fastest.
Arguments:
- qkv: bfloat16 [3, 32, 2, 512, 3072], P(None, 'dp', None, 'seq'), may hold values from -18 to 18
- cotangent: bfloat16 [32, 2, 512, 3072], P('dp', None, 'seq'), may hold values from -6 to 6
- lengths: int32 [32, 2], replicated, may hold values from 0 to 512, as said below
- target_group: int32 [32, 2], replicated, may hold values from 0 to 31, as said below
- target_slot: int32 [32, 2], replicated, may hold values from 0 to 1, as said below
Outputs:
- attended: bfloat16 [32, 2, 512, 3072], P('dp', None, 'seq')
- grad_qkv: bfloat16 [3, 32, 2, 512, 3072], P(None, 'dp', None, 'seq')
The draws below stay inside these ranges and needn't reach their ends.
Inputs may be any that keep to these rules, and one draw needn't show every extreme that they name: Each group holds 0 to 2 clips; an empty slot has length 0, a clip has 128 to 512 tokens, and some clip has exactly 512. A move lowers the larger of the two groups' sums of squared clip lengths. `target_group`: A clip stays in its group or moves to the group one below or one above; a group sends at most one clip to each neighbour and at most one clip arrives in a group; a group that sends receives nothing; group 0 sends one clip to group 1 and the last group one to the group below it; empty slots name their own group. `target_slot`: A clip that stays keeps its slot; a moving clip lands in a slot of its destination that holds no clip before the moves; empty slots name their own slot.
All inputs are finite; a program needn't handle non-finite values.
Results may differ from the reference program's by a relative error of at most 0.0049.
Values may be sent and summed in bfloat16 or wider, within the bound.
No kernel may reach another device: no remote copies, remote signals or barrier semaphores. Data moves between devices by JAX's collectives and lax.ppermute only.
A program may use at most 64 MiB of HBM per device.

```python
import jax
import jax.numpy as jnp
from jax import lax

HEADS = 24
HEAD = 128
CAP = 512
SLOTS = 2
GROUPS = 32


def clip_plan(key):
    subkeys = jax.random.split(key, 5)
    group_numbers = jnp.arange(GROUPS, dtype=jnp.int32)
    level = jax.random.randint(subkeys[0], (GROUPS,), 0, 8)
    clips = jnp.where(level < 1, 0, jnp.where(level < 4, 1, 2)).astype(jnp.int32)
    clips = clips.at[0].set(2).at[1].set(1).at[GROUPS - 3].set(1).at[GROUPS - 2].set(1).at[GROUPS - 1].set(2)
    coin_flips = jax.random.randint(subkeys[1], (GROUPS,), 0, 4)
    coin_flips = coin_flips.at[0].set(1).at[GROUPS - 1].set(3)
    clips_above = jnp.concatenate([clips[1:], jnp.zeros((1,), jnp.int32)])
    clips_below = jnp.concatenate([jnp.zeros((1,), jnp.int32), clips[:-1]])

    def advance(carry, inputs):
        taken_below, taken_here = carry
        own_clips, upper_clips, lower_clips, coin_value, group_number = inputs
        can_up = (own_clips == 2) & (group_number + 1 < GROUPS) & (upper_clips == 1)
        can_down = (own_clips == 2) & (group_number > 0) & (lower_clips == 1) & (taken_below == 0)
        prefer_up = jnp.where(can_up, 1, jnp.where(can_down, -1, 0))
        prefer_down = jnp.where(can_down, -1, jnp.where(can_up, 1, 0))
        direction = jnp.where(coin_value == 3, prefer_down, prefer_up).astype(jnp.int32)
        return ((taken_here, (direction == 1).astype(jnp.int32)), direction)
    initial = (jnp.zeros((), jnp.int32), jnp.zeros((), jnp.int32))
    _, directions = lax.scan(advance, initial, (clips, clips_above, clips_below, coin_flips, group_numbers))
    single = jax.random.randint(subkeys[3], (GROUPS,), 0, SLOTS)
    slot_numbers = jnp.arange(SLOTS, dtype=jnp.int32)[None, :]
    occupied = jnp.where(clips[:, None] == 2, True, jnp.where(clips[:, None] == 1, slot_numbers == single[:, None], False))
    long_sizes = jax.random.randint(subkeys[4], (GROUPS, SLOTS), CAP // 2, CAP + 1)
    short_sizes = jax.random.randint(subkeys[2], (GROUPS, SLOTS), CAP // 4, CAP // 2)
    sizes = jnp.where(clips[:, None] == 2, long_sizes, short_sizes)
    sizes = jnp.where(occupied, sizes, 0)
    sizes = sizes.at[0, 0].set(CAP).astype(jnp.int32)
    moving_slot = jnp.where(sizes[:, 1] < sizes[:, 0], 1, 0).astype(jnp.int32)
    moving = occupied & (clips[:, None] == 2) & (slot_numbers == moving_slot[:, None]) & (directions[:, None] != 0)
    destination = group_numbers + directions
    clamped = jnp.clip(destination, 0, GROUPS - 1)
    free_slot = SLOTS - 1 - single
    target_group = jnp.where(moving, destination[:, None], jnp.broadcast_to(group_numbers[:, None], (GROUPS, SLOTS)))
    target_slot = jnp.where(moving, free_slot[clamped][:, None], jnp.broadcast_to(slot_numbers, (GROUPS, SLOTS)))
    return (sizes, target_group.astype(jnp.int32), target_slot.astype(jnp.int32))


def draw_lengths(key, part):
    drawn_plan = clip_plan(key)
    return drawn_plan[0]


def draw_target_group(key, part):
    drawn_plan = clip_plan(key)
    return drawn_plan[1]


def draw_target_slot(key, part):
    drawn_plan = clip_plan(key)
    return drawn_plan[2]


def draw_qkv(key, part):
    key = jax.random.fold_in(key, 7)
    subkeys = jax.random.split(key, 1)
    features = HEADS * HEAD
    extents = (3, GROUPS, SLOTS, CAP, features)
    array_scale = jnp.array([2.5, 1.0, 1.0], jnp.float32).reshape(3, 1, 1, 1, 1)
    values = jax.random.truncated_normal(subkeys[0], -6.0, 6.0, extents, jnp.float32) * array_scale
    return values.astype(jnp.bfloat16)


def level_of(own_key, shape, shards, low, top_value):
    loudness, own = 1.0, jax.random.fold_in(own_key, 6)
    for axis_at, blocks in shards:
        heights = jnp.exp(jax.random.uniform(jax.random.fold_in(own, axis_at), (blocks,), jnp.float32, low / len(shards), top_value / len(shards)))
        loudness = loudness * jnp.repeat(heights, shape[axis_at] // blocks).reshape([-1 if axis == axis_at else 1 for axis in range(len(shape))])
    return loudness


def scatter_about(stream_key, shape, spread, reach, cuts=(), kind=jnp.bfloat16):
    gain = level_of(stream_key, shape, cuts, -0.22, 0.18) if cuts else 1.0
    values = jax.random.normal(stream_key, shape, jnp.float32) * spread * gain
    return jnp.minimum(jnp.maximum(values, -reach), reach).astype(kind)


def setup_inputs(seed: int = 0) -> dict:
    key_of = jax.random.split(jax.random.key(seed), 6)
    return {
        "qkv": draw_qkv(jax.random.fold_in(key_of[5], 71), 0),
        "cotangent": scatter_about(key_of[1], (GROUPS, SLOTS, CAP, HEADS * HEAD), 1.0, 6.0, ((0, 32), (2, 8))),
        "lengths": draw_lengths(jax.random.fold_in(key_of[5], 71), 0),
        "target_group": draw_target_group(jax.random.fold_in(key_of[5], 71), 0),
        "target_slot": draw_target_slot(jax.random.fold_in(key_of[5], 71), 0),
    }


def clip_pass(packed, upstream, count):
    extent = packed.shape[1]
    features = packed.shape[2]
    head_count = features // HEAD
    factor = HEAD ** -0.5
    queries = packed[0].astype(jnp.float32).reshape(extent, head_count, HEAD)
    key_heads = packed[1].astype(jnp.float32).reshape(extent, head_count, HEAD)
    value_heads = packed[2].astype(jnp.float32).reshape(extent, head_count, HEAD)
    scores = jnp.einsum("qhd,khd->hqk", queries, key_heads) * factor
    position = jnp.arange(extent)
    scores = jnp.where(position[None, None, :] < count, scores, -1.0e30)
    largest = jnp.max(scores, axis=2, keepdims=True)
    exponent = jnp.exp(scores - largest)
    weights = exponent / jnp.sum(exponent, axis=2, keepdims=True)
    rounded = lax.optimization_barrier(weights.astype(jnp.bfloat16)).astype(jnp.float32)
    inside = (position < count)[:, None, None]
    output = jnp.einsum("hqk,khd->qhd", rounded, value_heads)
    output = jnp.where(inside, output, 0.0).astype(jnp.bfloat16).reshape(extent, features)
    grad_rows = jnp.where(inside, upstream.astype(jnp.float32).reshape(extent, head_count, HEAD), 0.0)
    grad_weights = jnp.einsum("qhd,khd->hqk", grad_rows, value_heads)
    inner_sum = jnp.sum(grad_weights * weights, axis=2, keepdims=True)
    score_grad = weights * (grad_weights - inner_sum)
    rounded_grad = lax.optimization_barrier(score_grad.astype(jnp.bfloat16)).astype(jnp.float32)
    grad_q = (jnp.einsum("hqk,khd->qhd", rounded_grad, key_heads) * factor).astype(jnp.bfloat16)
    grad_k = (jnp.einsum("hqk,qhd->khd", rounded_grad, queries) * factor).astype(jnp.bfloat16)
    grad_v = jnp.einsum("hqk,qhd->khd", rounded, grad_rows).astype(jnp.bfloat16)
    gradients = jnp.stack([grad_q, grad_k, grad_v]).reshape(3, extent, features)
    return output, gradients


def reference(qkv, cotangent, lengths, target_group, target_slot):
    groups = lengths.shape[0]
    slot_count = lengths.shape[1]
    extent = qkv.shape[3]
    features = qkv.shape[4]
    home_grad = cotangent[target_group, target_slot]
    flat_qkv = jnp.moveaxis(qkv, 0, 2).reshape(groups * slot_count, 3, extent, features)

    def per_clip(bundle):
        return clip_pass(bundle[0], bundle[1], bundle[2])

    outputs, gradients = lax.map(per_clip, (flat_qkv, home_grad.reshape(groups * slot_count, extent, features), lengths.reshape(-1)))
    attended = jnp.zeros((groups, slot_count, extent, features), jnp.float32)
    attended = attended.at[target_group.reshape(-1), target_slot.reshape(-1)].add(outputs.astype(jnp.float32))
    attended = attended.astype(jnp.bfloat16)
    grad_qkv = jnp.moveaxis(gradients.reshape(groups, slot_count, 3, extent, features), 2, 0)
    return attended, grad_qkv
```

```python
import functools

import jax
import jax.numpy as jnp
from jax import lax
from jax.experimental import pallas as pl
from jax.experimental.pallas import tpu as pltpu
from jax.sharding import PartitionSpec as P

HEAD = 128
SEQ = 8
NEGATIVE = -1e30
LOG2E = 1.4426950408889634
ORDER = (4, 5, 2, 6, 3, 7, 1)
ANY = pl.BlockSpec(memory_space=pl.ANY)
SMEM = pl.BlockSpec(memory_space=pltpu.SMEM)


def run_all(copies):
    for copy in copies:
        copy.start()
    for copy in copies:
        copy.wait()


def column_block(k, width):
    other = lax.bitwise_xor(lax.axis_index("seq"), jnp.int32(k))
    return pl.ds(pl.multiple_of(other * width, 128), width)


def partners(group):
    odd = lax.rem(group, 2)
    return group + 1 - 2 * odd, group - 1 + 2 * odd


def plan_kernel(lengths, to_group, to_slot, plan):
    groups = lengths.shape[0]
    me = lax.axis_index("dp")
    grad_source = [jnp.int32(0), jnp.int32(0)]
    out_source = []
    for slot in range(2):
        stays = (lengths[me, slot] > 0) & (to_group[me, slot] == me)
        out_source.append(jnp.where(stays, 0, 3))
    for number, other in enumerate(partners(me)):
        inside = (other >= 0) & (other < groups)
        there = jnp.clip(other, 0, groups - 1)
        flag = jnp.int32(0)
        give_grad = jnp.int32(0)
        give_out = jnp.int32(0)
        for slot in range(2):
            leaves = inside & (lengths[me, slot] > 0) & (to_group[me, slot] == other)
            arrives = inside & (lengths[there, slot] > 0) & (to_group[there, slot] == me)
            lands = to_slot[there, slot]
            flag = jnp.where(leaves | arrives, 1, flag)
            give_grad = jnp.where(arrives, lands, give_grad)
            give_out = jnp.where(leaves, slot, give_out)
            grad_source[slot] = jnp.where(leaves, number + 1, grad_source[slot])
            for here in range(2):
                out_source[here] = jnp.where(arrives & (lands == here), number + 1, out_source[here])
        plan[3 * number] = flag
        plan[3 * number + 1] = give_grad
        plan[3 * number + 2] = give_out
    for slot in range(2):
        plan[6 + slot] = grad_source[slot]
        plan[8 + slot] = out_source[slot]
        plan[10 + slot] = lengths[me, slot]


def make_plan(lengths, to_group, to_slot):
    return pl.pallas_call(
        plan_kernel,
        out_shape=jax.ShapeDtypeStruct((12,), jnp.int32),
        in_specs=[SMEM] * 3,
        out_specs=SMEM,
        name="plan",
    )(lengths, to_group, to_slot)


def pack_qkv_kernel(qkv, *refs):
    outs, sem = refs[:SEQ], refs[SEQ]
    width = outs[0].shape[-1]
    run_all(
        [
            pltpu.make_async_copy(qkv.at[:, 0, :, :, column_block(k, width)], outs[k], sem.at[k])
            for k in range(SEQ)
        ]
    )


def pack_qkv(qkv):
    three, _, slots, rows, features = qkv.shape
    width = features // SEQ
    shape = jax.ShapeDtypeStruct((three, slots, rows, width), qkv.dtype)
    return pl.pallas_call(
        pack_qkv_kernel,
        out_shape=[shape] * SEQ,
        in_specs=[ANY],
        out_specs=[ANY] * SEQ,
        scratch_shapes=[pltpu.SemaphoreType.DMA((SEQ,))],
        name="pack_qkv",
    )(qkv)


def pack_grad_kernel(plan, own, even, odd, *refs):
    outs, sem = refs[:SEQ], refs[SEQ]
    width = outs[0].shape[-1]
    for slot in range(2):
        for choice, source in ((0, own.at[0, slot]), (1, even), (2, odd)):

            @pl.when(plan[6 + slot] == choice)
            def _(slot=slot, source=source):
                run_all(
                    [
                        pltpu.make_async_copy(
                            source.at[:, column_block(k, width)], outs[k].at[slot], sem.at[k]
                        )
                        for k in range(SEQ)
                    ]
                )


def pack_grad(plan, own, even, odd):
    _, slots, rows, features = own.shape
    width = features // SEQ
    shape = jax.ShapeDtypeStruct((slots, rows, width), own.dtype)
    return pl.pallas_call(
        pack_grad_kernel,
        out_shape=[shape] * SEQ,
        in_specs=[SMEM, ANY, ANY, ANY],
        out_specs=[ANY] * SEQ,
        scratch_shapes=[pltpu.SemaphoreType.DMA((SEQ,))],
        name="pack_grad",
    )(plan, own, even, odd)


def token_numbers(shape, axis):
    rows = shape[axis] // SEQ
    index = lax.broadcasted_iota(jnp.int32, shape, axis)
    block = lax.bitwise_xor(index // rows, lax.axis_index("seq"))
    return block * rows + lax.rem(index, rows)


def gathered(refs, array, head):
    columns = slice(head * HEAD, (head + 1) * HEAD)
    return jnp.concatenate([ref[array, 0, :, columns] for ref in refs], axis=0)


def dot(a, b, a_axis, b_axis):
    return lax.dot_general(
        a, b, (((a_axis,), (b_axis,)), ((), ())), preferred_element_type=jnp.float32
    )


def scores_of(queries, keys, valid_keys):
    scores = dot(keys, queries, 1, 1) * (HEAD**-0.5 * LOG2E)
    return jnp.where(valid_keys, scores, NEGATIVE)


def forward_kernel(plan, *refs):
    qkv, outs, stats = refs[:SEQ], refs[SEQ : 2 * SEQ], refs[2 * SEQ]
    rows = outs[0].shape[1]
    tokens = rows * SEQ
    heads = outs[0].shape[2] // HEAD
    count = plan[10 + pl.program_id(0)]

    @pl.when(count == 0)
    def _():
        for out in outs:
            out[...] = jnp.zeros_like(out)
        stats[...] = jnp.zeros_like(stats)

    @pl.when(count > 0)
    def _():
        valid_keys = token_numbers((tokens, tokens), 0) < count
        valid_queries = token_numbers((tokens, HEAD), 0) < count
        for head in range(heads):
            queries, keys, values = (gathered(qkv, array, head) for array in range(3))
            scores = scores_of(queries, keys, valid_keys)
            largest = jnp.max(scores, axis=0, keepdims=True)
            exponent = jnp.exp2(scores - largest)
            inverse = 1.0 / jnp.sum(exponent, axis=0, keepdims=True)
            weights = (exponent * inverse).astype(jnp.bfloat16)
            output = dot(values, weights, 0, 0).T
            output = jnp.where(valid_queries, output, 0.0).astype(jnp.bfloat16)
            for k, out in enumerate(outs):
                out[0, :, head * HEAD : (head + 1) * HEAD] = output[k * rows : (k + 1) * rows]
            stats[0, head : head + 1, :] = largest
            stats[0, heads + head : heads + head + 1, :] = inverse


def vmem_blocks(shape, slot_axis):
    block = tuple(1 if axis == slot_axis else size for axis, size in enumerate(shape))
    index = lambda slot: tuple(slot if axis == slot_axis else 0 for axis in range(len(shape)))
    return pl.BlockSpec(block, index)


def forward(plan, qkv):
    three, slots, rows, width = qkv[0].shape
    tokens = rows * SEQ
    out_shape = (slots, rows, width)
    stats_shape = (slots, 8, tokens)
    *outs, stats = pl.pallas_call(
        forward_kernel,
        grid=(slots,),
        out_shape=[jax.ShapeDtypeStruct(out_shape, jnp.bfloat16)] * SEQ
        + [jax.ShapeDtypeStruct(stats_shape, jnp.float32)],
        in_specs=[SMEM] + [vmem_blocks(qkv[0].shape, 1)] * SEQ,
        out_specs=[vmem_blocks(out_shape, 0)] * SEQ + [vmem_blocks(stats_shape, 0)],
        compiler_params=pltpu.CompilerParams(vmem_limit_bytes=40 << 20),
        name="forward",
    )(plan, *qkv)
    return outs, stats


def backward_kernel(plan, *refs):
    qkv, grads, stats, outs = (
        refs[:SEQ],
        refs[SEQ : 2 * SEQ],
        refs[2 * SEQ],
        refs[2 * SEQ + 1 :],
    )
    rows = grads[0].shape[1]
    tokens = rows * SEQ
    heads = grads[0].shape[2] // HEAD
    count = plan[10 + pl.program_id(0)]

    @pl.when(count == 0)
    def _():
        for out in outs:
            out[...] = jnp.zeros_like(out)

    @pl.when(count > 0)
    def _():
        valid_keys = token_numbers((tokens, tokens), 0) < count
        valid_queries = token_numbers((tokens, HEAD), 0) < count
        for head in range(heads):
            columns = slice(head * HEAD, (head + 1) * HEAD)
            queries, keys, values = (gathered(qkv, array, head) for array in range(3))
            upstream = jnp.concatenate([grad[0, :, columns] for grad in grads], axis=0)
            upstream = jnp.where(valid_queries, upstream, jnp.zeros_like(upstream))
            scores = scores_of(queries, keys, valid_keys)
            largest = stats[0, head : head + 1, :]
            inverse = stats[0, heads + head : heads + head + 1, :]
            weights = jnp.exp2(scores - largest) * inverse
            grad_values = dot(weights.astype(jnp.bfloat16), upstream, 1, 0)
            grad_weights = dot(values, upstream, 1, 1)
            inner = jnp.sum(grad_weights * weights, axis=0, keepdims=True)
            score_grad = (weights * (grad_weights - inner)).astype(jnp.bfloat16)
            factor = HEAD**-0.5
            grad_queries = dot(keys, score_grad, 0, 0).T * factor
            grad_keys = dot(score_grad, queries, 1, 0) * factor
            for array, grad in enumerate((grad_queries, grad_keys, grad_values)):
                grad = grad.astype(jnp.bfloat16)
                for k, out in enumerate(outs):
                    out[array, 0, :, columns] = grad[k * rows : (k + 1) * rows]


def backward(plan, qkv, grads, stats):
    return pl.pallas_call(
        backward_kernel,
        grid=(grads[0].shape[0],),
        out_shape=[jax.ShapeDtypeStruct(qkv[0].shape, jnp.bfloat16)] * SEQ,
        in_specs=[SMEM]
        + [vmem_blocks(qkv[0].shape, 1)] * SEQ
        + [vmem_blocks(grads[0].shape, 0)] * SEQ
        + [vmem_blocks(stats.shape, 0)],
        out_specs=[vmem_blocks(qkv[0].shape, 1)] * SEQ,
        compiler_params=pltpu.CompilerParams(vmem_limit_bytes=48 << 20),
        name="backward",
    )(plan, *qkv, *grads, stats)


def unpack_out_kernel(*refs):
    parts, out, sem = refs[:SEQ], refs[SEQ], refs[SEQ + 1]
    width = parts[0].shape[-1]
    run_all(
        [
            pltpu.make_async_copy(parts[k], out.at[:, :, column_block(k, width)], sem.at[k])
            for k in range(SEQ)
        ]
    )


def unpack_out(parts):
    slots, rows, width = parts[0].shape
    return pl.pallas_call(
        unpack_out_kernel,
        out_shape=jax.ShapeDtypeStruct((slots, rows, width * SEQ), parts[0].dtype),
        in_specs=[ANY] * SEQ,
        out_specs=ANY,
        scratch_shapes=[pltpu.SemaphoreType.DMA((SEQ,))],
        name="unpack_out",
    )(*parts)


def place_kernel(plan, own, even, odd, out, zeros, sem):
    zeros[...] = jnp.zeros_like(zeros)
    for slot in range(2):
        for choice, source in ((0, own.at[slot]), (1, even), (2, odd), (3, zeros)):

            @pl.when(plan[8 + slot] == choice)
            def _(slot=slot, source=source):
                run_all([pltpu.make_async_copy(source, out.at[0, slot], sem.at[0])])


def place(plan, own, even, odd):
    slots, rows, features = own.shape
    return pl.pallas_call(
        place_kernel,
        out_shape=jax.ShapeDtypeStruct((1, slots, rows, features), own.dtype),
        in_specs=[SMEM, ANY, ANY, ANY],
        out_specs=ANY,
        scratch_shapes=[pltpu.VMEM((rows, features), own.dtype), pltpu.SemaphoreType.DMA((1,))],
        name="place",
    )(plan, own, even, odd)


def unpack_grads_kernel(*refs):
    parts, out, sem = refs[:SEQ], refs[SEQ], refs[SEQ + 1]
    width = parts[0].shape[-1]
    run_all(
        [
            pltpu.make_async_copy(parts[k], out.at[:, 0, :, :, column_block(k, width)], sem.at[k])
            for k in range(SEQ)
        ]
    )


def unpack_grads(parts):
    three, slots, rows, width = parts[0].shape
    return pl.pallas_call(
        unpack_grads_kernel,
        out_shape=jax.ShapeDtypeStruct((three, 1, slots, rows, width * SEQ), parts[0].dtype),
        in_specs=[ANY] * SEQ,
        out_specs=ANY,
        scratch_shapes=[pltpu.SemaphoreType.DMA((SEQ,))],
        name="unpack_grads",
    )(*parts)


def exchange(parts):
    received = list(parts)
    for k in ORDER:
        received[k] = lax.ppermute(parts[k], "seq", [(i, i ^ k) for i in range(SEQ)])
    return received


def swap(flag, slot, slots, first, groups):
    pairs = []
    for low in range(first, groups - 1, 2):
        pairs += [(low, low + 1), (low + 1, low)]

    def move(slots, slot):
        return lax.ppermute(lax.dynamic_index_in_dim(slots, slot, 0, keepdims=False), "dp", pairs)

    def stay(slots, slot):
        return jnp.zeros(slots.shape[1:], slots.dtype)

    return lax.cond(flag > 0, move, stay, slots, slot)


def on_device(qkv, cotangent, lengths, to_group, to_slot):
    groups = lengths.shape[0]
    plan = make_plan(lengths, to_group, to_slot)
    qkv_parts = exchange(pack_qkv(qkv))
    even, odd = (
        swap(plan[3 * n], plan[3 * n + 1], cotangent[0], n, groups) for n in range(2)
    )
    grad_parts = exchange(pack_grad(plan, cotangent, even, odd))
    out_parts, stats = forward(plan, qkv_parts)
    home_out = unpack_out(exchange(out_parts))
    grads = exchange(backward(plan, qkv_parts, grad_parts, stats))
    even, odd = (swap(plan[3 * n], plan[3 * n + 2], home_out, n, groups) for n in range(2))
    attended = place(plan, home_out, even, odd)
    return attended, unpack_grads(grads)


def solution(mesh):
    in_specs = (P(None, "dp", None, "seq", None), P("dp", None, "seq", None), P(), P(), P())
    out_specs = (P("dp", None, "seq", None), P(None, "dp", None, "seq", None))
    return jax.shard_map(
        on_device, mesh=mesh, in_specs=in_specs, out_specs=out_specs, check_vma=False
    )
```

```python
import functools

import jax
import jax.numpy as jnp
from jax import lax
from jax.experimental import pallas as pl
from jax.experimental.pallas import tpu as pltpu
from jax.sharding import PartitionSpec as P

HEAD = 128
SEQ = 8
ARRAYS = 4
NEGATIVE = -1e30
LOG2E = 1.4426950408889634
ORDER = (2, 6, 4, 3, 7, 5, 1)
CHUNKS = ((0, 1), (1, 2))
ANY = pl.BlockSpec(memory_space=pl.ANY)
VMEM = pl.BlockSpec(memory_space=pltpu.VMEM)
SMEM = pl.BlockSpec(memory_space=pltpu.SMEM)


def partners(group):
    odd = lax.rem(group, 2)
    return group + 1 - 2 * odd, group - 1 + 2 * odd


def plan_kernel(lengths, to_group, to_slot, plan):
    groups = lengths.shape[0]
    me = lax.axis_index("dp")
    grad_source = [jnp.int32(0), jnp.int32(0)]
    out_source = []
    for slot in range(2):
        stays = (lengths[me, slot] > 0) & (to_group[me, slot] == me)
        out_source.append(jnp.where(stays, 0, 3))
    for number, other in enumerate(partners(me)):
        inside = (other >= 0) & (other < groups)
        there = jnp.clip(other, 0, groups - 1)
        kind = jnp.int32(0)
        given = jnp.int32(0)
        for slot in range(2):
            leaves = inside & (lengths[me, slot] > 0) & (to_group[me, slot] == other)
            arrives = inside & (lengths[there, slot] > 0) & (to_group[there, slot] == me)
            lands = to_slot[there, slot]
            kind = jnp.where(leaves, 1, jnp.where(arrives, 2, kind))
            given = jnp.where(leaves, slot, jnp.where(arrives, lands, given))
            grad_source[slot] = jnp.where(leaves, number + 1, grad_source[slot])
            for here in range(2):
                out_source[here] = jnp.where(arrives & (lands == here), number + 1, out_source[here])
        plan[2 * number] = kind
        plan[2 * number + 1] = given
    for slot in range(2):
        plan[4 + slot] = grad_source[slot]
        plan[6 + slot] = out_source[slot]
        plan[8 + slot] = lengths[me, slot]


def make_plan(lengths, to_group, to_slot):
    return pl.pallas_call(
        plan_kernel,
        out_shape=jax.ShapeDtypeStruct((10,), jnp.int32),
        in_specs=[SMEM] * 3,
        out_specs=SMEM,
        name="plan",
    )(lengths, to_group, to_slot)


def block_columns(k, device_width, chunk):
    other = lax.bitwise_xor(lax.axis_index("seq"), jnp.int32(k))
    start = pl.multiple_of(other * device_width + chunk[0] * HEAD, HEAD)
    return pl.ds(start, chunk[1] * HEAD)


def pack_kernel(chunk, qkv, cotangent, *refs):
    outs, (held, come, go) = refs[:SEQ], refs[SEQ:]
    device_width = qkv.shape[-1] // SEQ
    arrive = []
    for k in range(SEQ):
        columns = block_columns(k, device_width, chunk)
        arrive.append(
            (
                pltpu.make_async_copy(
                    qkv.at[:, 0, :, :, columns], held.at[k, pl.ds(0, 3)], come.at[k, 0]
                ),
                pltpu.make_async_copy(
                    cotangent.at[0, :, :, columns], held.at[k, 3], come.at[k, 1]
                ),
            )
        )
    leave = [pltpu.make_async_copy(held.at[k], outs[k], go.at[k]) for k in range(SEQ)]
    for pair in arrive:
        for copy in pair:
            copy.start()
    for pair, copy in zip(arrive, leave):
        for part in pair:
            part.wait()
        copy.start()
    for copy in leave:
        copy.wait()


def pack(qkv, cotangent, chunk):
    _, slots, rows, _ = cotangent.shape
    shape = (ARRAYS, slots, rows, chunk[1] * HEAD)
    return pl.pallas_call(
        functools.partial(pack_kernel, chunk),
        out_shape=[jax.ShapeDtypeStruct(shape, qkv.dtype)] * SEQ,
        in_specs=[ANY, ANY],
        out_specs=[ANY] * SEQ,
        scratch_shapes=[
            pltpu.VMEM((SEQ, *shape), qkv.dtype),
            pltpu.SemaphoreType.DMA((SEQ, 2)),
            pltpu.SemaphoreType.DMA((SEQ,)),
        ],
        name="pack",
    )(qkv, cotangent)


def exchange(parts):
    received = list(parts)
    for k in ORDER:
        received[k] = lax.ppermute(parts[k], "seq", [(i, i ^ k) for i in range(SEQ)])
    return received


def token_numbers(shape, axis):
    rows = shape[axis] // SEQ
    index = lax.broadcasted_iota(jnp.int32, shape, axis)
    block = lax.bitwise_xor(index // rows, lax.axis_index("seq"))
    return block * rows + lax.rem(index, rows)


def head_columns(head):
    return slice(head * HEAD, (head + 1) * HEAD)


def gathered(parts, array, slot, columns):
    return jnp.concatenate([part[array, slot, :, columns] for part in parts], axis=0)


def dot(a, b, a_axis, b_axis):
    return lax.dot_general(
        a, b, (((a_axis,), (b_axis,)), ((), ())), preferred_element_type=jnp.float32
    )


def scores_of(queries, keys, valid_keys):
    scores = dot(keys, queries, 1, 1) * (HEAD**-0.5 * LOG2E)
    return jnp.where(valid_keys, scores, NEGATIVE)


def forward_kernel(plan, *refs):
    parts, (out, stats, *gifts) = refs[:SEQ], refs[SEQ:]
    slots, tokens, width = out.shape
    rows = tokens // SEQ
    heads = width // HEAD
    for slot in range(slots):
        count = plan[8 + slot]

        @pl.when(count == 0)
        def _():
            out[slot] = jnp.zeros_like(out[slot])

        @pl.when(count > 0)
        def _():
            valid_keys = token_numbers((tokens, tokens), 0) < count
            valid_queries = token_numbers((tokens, HEAD), 0) < count
            for head in range(heads):
                columns = head_columns(head)
                queries, keys, values = (gathered(parts, n, slot, columns) for n in range(3))
                scores = scores_of(queries, keys, valid_keys)
                largest = jnp.max(scores, axis=0, keepdims=True)
                exponent = jnp.exp2(scores - largest)
                inverse = 1.0 / jnp.sum(exponent, axis=0, keepdims=True)
                weights = (exponent * inverse).astype(jnp.bfloat16)
                output = dot(values, weights, 0, 0).T
                output = jnp.where(valid_queries, output, 0.0).astype(jnp.bfloat16)
                out[slot, :, columns] = output
                stats[slot, 2 * head : 2 * head + 1, :] = largest
                stats[slot, 2 * head + 1 : 2 * head + 2, :] = inverse

    for number, gift in enumerate(gifts):
        for slot in range(slots):
            chosen = plan[2 * number + 1] == slot

            @pl.when((plan[2 * number] == 1) & chosen)
            def _():
                gift[...] = out[slot]

            @pl.when((plan[2 * number] == 2) & chosen)
            def _():
                for k, part in enumerate(parts):
                    gift[k * rows : (k + 1) * rows] = part[3, slot]


def forward(plan, parts):
    _, slots, rows, width = parts[0].shape
    tokens = rows * SEQ
    gift = jax.ShapeDtypeStruct((tokens, width), jnp.bfloat16)
    return pl.pallas_call(
        forward_kernel,
        out_shape=[
            jax.ShapeDtypeStruct((slots, tokens, width), jnp.bfloat16),
            jax.ShapeDtypeStruct((slots, 8, tokens), jnp.float32),
            gift,
            gift,
        ],
        in_specs=[SMEM] + [VMEM] * SEQ,
        out_specs=[VMEM] * 4,
        compiler_params=pltpu.CompilerParams(vmem_limit_bytes=40 << 20),
        name="forward",
    )(plan, *parts)


def backward_kernel(plan, *refs):
    parts, (home_out, stats, even, odd), outs = refs[:SEQ], refs[SEQ : SEQ + 4], refs[SEQ + 4 :]
    slots, tokens, width = home_out.shape
    rows = tokens // SEQ
    heads = width // HEAD
    for slot in range(slots):
        count = plan[8 + slot]
        for choice, source in ((0, home_out.at[slot]), (1, even), (2, odd)):

            @pl.when(plan[6 + slot] == choice)
            def _():
                for k, out in enumerate(outs):
                    out[0, slot] = source[k * rows : (k + 1) * rows]

        @pl.when(plan[6 + slot] == 3)
        def _():
            for out in outs:
                out[0, slot] = jnp.zeros_like(out[0, slot])

        @pl.when(count == 0)
        def _():
            for out in outs:
                for array in range(1, ARRAYS):
                    out[array, slot] = jnp.zeros_like(out[array, slot])

        @pl.when(count > 0)
        def _():
            source = plan[4 + slot]
            valid_keys = token_numbers((tokens, tokens), 0) < count
            valid_queries = token_numbers((tokens, HEAD), 0) < count
            factor = HEAD**-0.5
            for head in range(heads):
                columns = head_columns(head)
                queries, keys, values, own = (
                    gathered(parts, n, slot, columns) for n in range(ARRAYS)
                )
                moved = jnp.where(source == 1, even[:, columns], odd[:, columns])
                upstream = jnp.where(source == 0, own, moved)
                upstream = jnp.where(valid_queries, upstream, jnp.zeros_like(upstream))
                scores = scores_of(queries, keys, valid_keys)
                largest = stats[slot, 2 * head : 2 * head + 1, :]
                inverse = stats[slot, 2 * head + 1 : 2 * head + 2, :]
                weights = jnp.exp2(scores - largest) * inverse
                grad_values = dot(weights.astype(jnp.bfloat16), upstream, 1, 0)
                grad_weights = dot(values, upstream, 1, 1)
                inner = jnp.sum(grad_weights * weights, axis=0, keepdims=True)
                score_grad = (weights * (grad_weights - inner)).astype(jnp.bfloat16)
                grad_queries = dot(keys, score_grad, 0, 0).T * factor
                grad_keys = dot(score_grad, queries, 1, 0) * factor
                for n, grad in enumerate((grad_queries, grad_keys, grad_values)):
                    grad = grad.astype(jnp.bfloat16)
                    for k, out in enumerate(outs):
                        out[1 + n, slot, :, columns] = grad[k * rows : (k + 1) * rows]


def backward(plan, parts, home_out, stats, even, odd):
    return pl.pallas_call(
        backward_kernel,
        out_shape=[jax.ShapeDtypeStruct(parts[0].shape, jnp.bfloat16)] * SEQ,
        in_specs=[SMEM] + [VMEM] * (SEQ + 4),
        out_specs=[VMEM] * SEQ,
        compiler_params=pltpu.CompilerParams(vmem_limit_bytes=48 << 20),
        name="backward",
    )(plan, *parts, home_out, stats, even, odd)


def unpack_kernel(chunk, *refs):
    parts, (attended, grads, sem) = refs[:SEQ], refs[-3:]
    device_width = grads.shape[-1] // SEQ
    copies = []
    for k, part in enumerate(parts):
        columns = block_columns(k, device_width, chunk)
        copies += [
            pltpu.make_async_copy(part.at[0], attended.at[0, :, :, columns], sem.at[k, 0]),
            pltpu.make_async_copy(
                part.at[pl.ds(1, 3)], grads.at[:, 0, :, :, columns], sem.at[k, 1]
            ),
        ]
    for copy in copies:
        copy.start()
    for copy in copies:
        copy.wait()


def unpack(parts, chunk, device_heads, filled=()):
    _, slots, rows, _ = parts[0].shape
    features = device_heads * HEAD * SEQ
    return pl.pallas_call(
        functools.partial(unpack_kernel, chunk),
        out_shape=[
            jax.ShapeDtypeStruct((1, slots, rows, features), jnp.bfloat16),
            jax.ShapeDtypeStruct((3, 1, slots, rows, features), jnp.bfloat16),
        ],
        in_specs=[VMEM] * SEQ + [ANY] * len(filled),
        out_specs=[ANY, ANY],
        input_output_aliases={SEQ + n: n for n in range(len(filled))},
        scratch_shapes=[pltpu.SemaphoreType.DMA((SEQ, 2))],
        name="unpack",
    )(*parts, *filled)


def swap(kind, gift, first, groups):
    pairs = []
    for low in range(first, groups - 1, 2):
        pairs += [(low, low + 1), (low + 1, low)]
    return lax.cond(
        kind > 0, lambda gift: lax.ppermute(gift, "dp", pairs), lambda gift: gift, gift
    )


def after(value, *others):
    return lax.optimization_barrier((value, *others))[0]


def on_device(qkv, cotangent, lengths, to_group, to_slot):
    groups = lengths.shape[0]
    device_heads = qkv.shape[-1] // (HEAD * SEQ)
    plan = make_plan(lengths, to_group, to_slot)
    packed = [pack(qkv, cotangent, chunk) for chunk in CHUNKS]
    arrived = [exchange(parts) for parts in packed]
    returned = []
    for parts in arrived:
        home_out, stats, *gifts = forward(plan, parts)
        even, odd = (swap(plan[2 * n], gifts[n], n, groups) for n in range(2))
        returned.append(exchange(backward(plan, parts, home_out, stats, even, odd)))
    results = ()
    for parts, chunk in zip(returned, CHUNKS):
        results = unpack(parts, chunk, device_heads, results)
    return tuple(results)


def solution(mesh):
    in_specs = (P(None, "dp", None, "seq", None), P("dp", None, "seq", None), P(), P(), P())
    out_specs = (P("dp", None, "seq", None), P(None, "dp", None, "seq", None))
    return jax.shard_map(
        on_device, mesh=mesh, in_specs=in_specs, out_specs=out_specs, check_vma=False
    )
```

```python
import functools

import jax
import jax.numpy as jnp
from jax import lax
from jax.experimental import pallas as pl
from jax.experimental.pallas import tpu as pltpu
from jax.sharding import PartitionSpec as P

HEAD = 128
SEQ = 8
ARRAYS = 4
NEGATIVE = -1e30
LOG2E = 1.4426950408889634
CORES = 2
ORDER = (4, 5, 2, 6, 3, 7, 1)
CHUNKS = ((0, 3),)
ANY = pl.BlockSpec(memory_space=pl.ANY)
VMEM = pl.BlockSpec(memory_space=pltpu.VMEM)
SMEM = pl.BlockSpec(memory_space=pltpu.SMEM)


def partners(group):
    odd = lax.rem(group, 2)
    return group + 1 - 2 * odd, group - 1 + 2 * odd


def plan_kernel(lengths, to_group, to_slot, plan):
    groups = lengths.shape[0]
    me = lax.axis_index("dp")
    grad_source = [jnp.int32(0), jnp.int32(0)]
    out_source = []
    for slot in range(2):
        stays = (lengths[me, slot] > 0) & (to_group[me, slot] == me)
        out_source.append(jnp.where(stays, 0, 3))
    for number, other in enumerate(partners(me)):
        inside = (other >= 0) & (other < groups)
        there = jnp.clip(other, 0, groups - 1)
        kind = jnp.int32(0)
        given = jnp.int32(0)
        for slot in range(2):
            leaves = inside & (lengths[me, slot] > 0) & (to_group[me, slot] == other)
            arrives = inside & (lengths[there, slot] > 0) & (to_group[there, slot] == me)
            lands = to_slot[there, slot]
            kind = jnp.where(leaves, 1, jnp.where(arrives, 2, kind))
            given = jnp.where(leaves, slot, jnp.where(arrives, lands, given))
            grad_source[slot] = jnp.where(leaves, number + 1, grad_source[slot])
            for here in range(2):
                out_source[here] = jnp.where(arrives & (lands == here), number + 1, out_source[here])
        plan[2 * number] = kind
        plan[2 * number + 1] = given
    for slot in range(2):
        plan[4 + slot] = grad_source[slot]
        plan[6 + slot] = out_source[slot]
        plan[8 + slot] = lengths[me, slot]


def make_plan(lengths, to_group, to_slot):
    return pl.pallas_call(
        plan_kernel,
        out_shape=jax.ShapeDtypeStruct((10,), jnp.int32),
        in_specs=[SMEM] * 3,
        out_specs=SMEM,
        name="plan",
    )(lengths, to_group, to_slot)


def reached(seq, k, sign):
    chips = SEQ // CORES
    chip = (seq // CORES + sign * (k // CORES) + chips) % chips
    return chip * CORES + (seq + k) % CORES


def block_columns(k, device_width, chunk):
    other = reached(lax.axis_index("seq"), k, 1)
    start = pl.multiple_of(other * device_width + chunk[0] * HEAD, HEAD)
    return pl.ds(start, chunk[1] * HEAD)


def pack_kernel(chunk, qkv, cotangent, *refs):
    outs, (held, come, go) = refs[:SEQ], refs[SEQ:]
    device_width = qkv.shape[-1] // SEQ
    arrive = []
    for k in range(SEQ):
        columns = block_columns(k, device_width, chunk)
        arrive.append(
            (
                pltpu.make_async_copy(
                    qkv.at[:, 0, :, :, columns], held.at[k, pl.ds(0, 3)], come.at[k, 0]
                ),
                pltpu.make_async_copy(
                    cotangent.at[0, :, :, columns], held.at[k, 3], come.at[k, 1]
                ),
            )
        )
    leave = [pltpu.make_async_copy(held.at[k], outs[k], go.at[k]) for k in range(SEQ)]
    for pair in arrive:
        for copy in pair:
            copy.start()
    for pair, copy in zip(arrive, leave):
        for part in pair:
            part.wait()
        copy.start()
    for copy in leave:
        copy.wait()


def pack(qkv, cotangent, chunk):
    _, slots, rows, _ = cotangent.shape
    shape = (ARRAYS, slots, rows, chunk[1] * HEAD)
    return pl.pallas_call(
        functools.partial(pack_kernel, chunk),
        out_shape=[jax.ShapeDtypeStruct(shape, qkv.dtype)] * SEQ,
        in_specs=[ANY, ANY],
        out_specs=[ANY] * SEQ,
        scratch_shapes=[
            pltpu.VMEM((SEQ, *shape), qkv.dtype),
            pltpu.SemaphoreType.DMA((SEQ, 2)),
            pltpu.SemaphoreType.DMA((SEQ,)),
        ],
        name="pack",
    )(qkv, cotangent)


def exchange(parts, sign):
    received = list(parts)
    for k in ORDER:
        pairs = [(i, reached(i, k, sign)) for i in range(SEQ)]
        received[k] = lax.ppermute(parts[k], "seq", pairs)
    return received


def token_numbers(shape, axis):
    rows = shape[axis] // SEQ
    blocks = [reached(lax.axis_index("seq"), k, -1) for k in range(SEQ)]
    piece = shape[:axis] + (rows,) + shape[axis + 1 :]
    within = lax.broadcasted_iota(jnp.int32, piece, axis)
    return jnp.concatenate([within + block * rows for block in blocks], axis=axis)


def head_columns(head):
    return slice(head * HEAD, (head + 1) * HEAD)


def gathered(parts, array, slot, columns):
    return jnp.concatenate([part[array, slot, :, columns] for part in parts], axis=0)


def dot(a, b, a_axis, b_axis):
    return lax.dot_general(
        a, b, (((a_axis,), (b_axis,)), ((), ())), preferred_element_type=jnp.float32
    )


def scores_of(queries, keys, valid_keys):
    scores = dot(keys, queries, 1, 1) * (HEAD**-0.5 * LOG2E)
    return jnp.where(valid_keys, scores, NEGATIVE)


def forward_kernel(plan, *refs):
    parts, (out, stats, *gifts) = refs[:SEQ], refs[SEQ:]
    slots, tokens, width = out.shape
    rows = tokens // SEQ
    heads = width // HEAD
    for slot in range(slots):
        count = plan[8 + slot]

        @pl.when(count == 0)
        def _():
            out[slot] = jnp.zeros_like(out[slot])

        @pl.when(count > 0)
        def _():
            valid_keys = token_numbers((tokens, tokens), 0) < count
            valid_queries = token_numbers((tokens, HEAD), 0) < count
            for head in range(heads):
                columns = head_columns(head)
                queries, keys, values = (gathered(parts, n, slot, columns) for n in range(3))
                scores = scores_of(queries, keys, valid_keys)
                largest = jnp.max(scores, axis=0, keepdims=True)
                exponent = jnp.exp2(scores - largest)
                inverse = 1.0 / jnp.sum(exponent, axis=0, keepdims=True)
                weights = (exponent * inverse).astype(jnp.bfloat16)
                output = dot(values, weights, 0, 0).T
                output = jnp.where(valid_queries, output, 0.0).astype(jnp.bfloat16)
                out[slot, :, columns] = output
                stats[slot, 2 * head : 2 * head + 1, :] = largest
                stats[slot, 2 * head + 1 : 2 * head + 2, :] = inverse

    for number, gift in enumerate(gifts):
        for slot in range(slots):
            chosen = plan[2 * number + 1] == slot

            @pl.when((plan[2 * number] == 1) & chosen)
            def _():
                gift[...] = out[slot]

            @pl.when((plan[2 * number] == 2) & chosen)
            def _():
                for k, part in enumerate(parts):
                    gift[k * rows : (k + 1) * rows] = part[3, slot]


def forward(plan, parts):
    _, slots, rows, width = parts[0].shape
    tokens = rows * SEQ
    gift = jax.ShapeDtypeStruct((tokens, width), jnp.bfloat16)
    return pl.pallas_call(
        forward_kernel,
        out_shape=[
            jax.ShapeDtypeStruct((slots, tokens, width), jnp.bfloat16),
            jax.ShapeDtypeStruct((slots, 8, tokens), jnp.float32),
            gift,
            gift,
        ],
        in_specs=[SMEM] + [VMEM] * SEQ,
        out_specs=[VMEM] * 4,
        compiler_params=pltpu.CompilerParams(vmem_limit_bytes=40 << 20),
        name="forward",
    )(plan, *parts)


def backward_kernel(plan, *refs):
    parts, (home_out, stats, even, odd), outs = refs[:SEQ], refs[SEQ : SEQ + 4], refs[SEQ + 4 :]
    slots, tokens, width = home_out.shape
    rows = tokens // SEQ
    heads = width // HEAD
    for slot in range(slots):
        count = plan[8 + slot]
        for choice, source in ((0, home_out.at[slot]), (1, even), (2, odd)):

            @pl.when(plan[6 + slot] == choice)
            def _():
                for k, out in enumerate(outs):
                    out[0, slot] = source[k * rows : (k + 1) * rows]

        @pl.when(plan[6 + slot] == 3)
        def _():
            for out in outs:
                out[0, slot] = jnp.zeros_like(out[0, slot])

        @pl.when(count == 0)
        def _():
            for out in outs:
                for array in range(1, ARRAYS):
                    out[array, slot] = jnp.zeros_like(out[array, slot])

        @pl.when(count > 0)
        def _():
            source = plan[4 + slot]
            valid_keys = token_numbers((tokens, tokens), 0) < count
            valid_queries = token_numbers((tokens, HEAD), 0) < count
            factor = HEAD**-0.5
            for head in range(heads):
                columns = head_columns(head)
                queries, keys, values, own = (
                    gathered(parts, n, slot, columns) for n in range(ARRAYS)
                )
                moved = jnp.where(source == 1, even[:, columns], odd[:, columns])
                upstream = jnp.where(source == 0, own, moved)
                upstream = jnp.where(valid_queries, upstream, jnp.zeros_like(upstream))
                scores = scores_of(queries, keys, valid_keys)
                largest = stats[slot, 2 * head : 2 * head + 1, :]
                inverse = stats[slot, 2 * head + 1 : 2 * head + 2, :]
                weights = jnp.exp2(scores - largest) * inverse
                grad_values = dot(weights.astype(jnp.bfloat16), upstream, 1, 0)
                grad_weights = dot(values, upstream, 1, 1)
                inner = jnp.sum(grad_weights * weights, axis=0, keepdims=True)
                score_grad = (weights * (grad_weights - inner)).astype(jnp.bfloat16)
                grad_queries = dot(keys, score_grad, 0, 0).T * factor
                grad_keys = dot(score_grad, queries, 1, 0) * factor
                for n, grad in enumerate((grad_queries, grad_keys, grad_values)):
                    grad = grad.astype(jnp.bfloat16)
                    for k, out in enumerate(outs):
                        out[1 + n, slot, :, columns] = grad[k * rows : (k + 1) * rows]


def backward(plan, parts, home_out, stats, even, odd):
    return pl.pallas_call(
        backward_kernel,
        out_shape=[jax.ShapeDtypeStruct(parts[0].shape, jnp.bfloat16)] * SEQ,
        in_specs=[SMEM] + [VMEM] * (SEQ + 4),
        out_specs=[VMEM] * SEQ,
        compiler_params=pltpu.CompilerParams(vmem_limit_bytes=48 << 20),
        name="backward",
    )(plan, *parts, home_out, stats, even, odd)


def unpack_kernel(chunk, *refs):
    parts, (attended, grads, sem) = refs[:SEQ], refs[-3:]
    device_width = grads.shape[-1] // SEQ
    copies = []
    for k, part in enumerate(parts):
        columns = block_columns(k, device_width, chunk)
        copies += [
            pltpu.make_async_copy(part.at[0], attended.at[0, :, :, columns], sem.at[k, 0]),
            pltpu.make_async_copy(
                part.at[pl.ds(1, 3)], grads.at[:, 0, :, :, columns], sem.at[k, 1]
            ),
        ]
    for copy in copies:
        copy.start()
    for copy in copies:
        copy.wait()


def unpack(parts, chunk, device_heads, filled=()):
    _, slots, rows, _ = parts[0].shape
    features = device_heads * HEAD * SEQ
    return pl.pallas_call(
        functools.partial(unpack_kernel, chunk),
        out_shape=[
            jax.ShapeDtypeStruct((1, slots, rows, features), jnp.bfloat16),
            jax.ShapeDtypeStruct((3, 1, slots, rows, features), jnp.bfloat16),
        ],
        in_specs=[VMEM] * SEQ + [ANY] * len(filled),
        out_specs=[ANY, ANY],
        input_output_aliases={SEQ + n: n for n in range(len(filled))},
        scratch_shapes=[pltpu.SemaphoreType.DMA((SEQ, 2))],
        name="unpack",
    )(*parts, *filled)


def swap(kind, gift, first, groups):
    pairs = []
    for low in range(first, groups - 1, 2):
        pairs += [(low, low + 1), (low + 1, low)]
    return lax.cond(
        kind > 0, lambda gift: lax.ppermute(gift, "dp", pairs), lambda gift: gift, gift
    )


def after(value, *others):
    return lax.optimization_barrier((value, *others))[0]


def on_device(qkv, cotangent, lengths, to_group, to_slot):
    groups = lengths.shape[0]
    device_heads = qkv.shape[-1] // (HEAD * SEQ)
    plan = make_plan(lengths, to_group, to_slot)
    packed = [pack(qkv, cotangent, chunk) for chunk in CHUNKS]
    arrived = [exchange(parts, 1) for parts in packed]
    returned = []
    for parts in arrived:
        home_out, stats, *gifts = forward(plan, parts)
        even, odd = (swap(plan[2 * n], gifts[n], n, groups) for n in range(2))
        returned.append(exchange(backward(plan, parts, home_out, stats, even, odd), -1))
    results = ()
    for parts, chunk in zip(returned, CHUNKS):
        results = unpack(parts, chunk, device_heads, results)
    return tuple(results)


def solution(mesh):
    in_specs = (P(None, "dp", None, "seq", None), P("dp", None, "seq", None), P(), P(), P())
    out_specs = (P("dp", None, "seq", None), P(None, "dp", None, "seq", None))
    return jax.shard_map(
        on_device, mesh=mesh, in_specs=in_specs, out_specs=out_specs, check_vma=False
    )
```

```python
import functools

import jax
import jax.numpy as jnp
from jax import lax
from jax.experimental import pallas as pl
from jax.experimental.pallas import tpu as pltpu
from jax.sharding import PartitionSpec as P

HEAD = 128
SEQ = 8
ARRAYS = 4
NEGATIVE = -1e30
LOG2E = 1.4426950408889634
CORES = 2
ORDER = (4, 6, 5, 7, 2, 3, 1)
CHUNKS = ((0, 3),)
ANY = pl.BlockSpec(memory_space=pl.ANY)
VMEM = pl.BlockSpec(memory_space=pltpu.VMEM)
SMEM = pl.BlockSpec(memory_space=pltpu.SMEM)


def partners(group):
    odd = lax.rem(group, 2)
    return group + 1 - 2 * odd, group - 1 + 2 * odd


def plan_kernel(lengths, to_group, to_slot, plan):
    groups = lengths.shape[0]
    me = lax.axis_index("dp")
    grad_source = [jnp.int32(0), jnp.int32(0)]
    out_source = []
    for slot in range(2):
        stays = (lengths[me, slot] > 0) & (to_group[me, slot] == me)
        out_source.append(jnp.where(stays, 0, 3))
    for number, other in enumerate(partners(me)):
        inside = (other >= 0) & (other < groups)
        there = jnp.clip(other, 0, groups - 1)
        kind = jnp.int32(0)
        given = jnp.int32(0)
        for slot in range(2):
            leaves = inside & (lengths[me, slot] > 0) & (to_group[me, slot] == other)
            arrives = inside & (lengths[there, slot] > 0) & (to_group[there, slot] == me)
            lands = to_slot[there, slot]
            kind = jnp.where(leaves, 1, jnp.where(arrives, 2, kind))
            given = jnp.where(leaves, slot, jnp.where(arrives, lands, given))
            grad_source[slot] = jnp.where(leaves, number + 1, grad_source[slot])
            for here in range(2):
                out_source[here] = jnp.where(arrives & (lands == here), number + 1, out_source[here])
        plan[2 * number] = kind
        plan[2 * number + 1] = given
    for slot in range(2):
        plan[4 + slot] = grad_source[slot]
        plan[6 + slot] = out_source[slot]
        plan[8 + slot] = lengths[me, slot]


def make_plan(lengths, to_group, to_slot):
    return pl.pallas_call(
        plan_kernel,
        out_shape=jax.ShapeDtypeStruct((10,), jnp.int32),
        in_specs=[SMEM] * 3,
        out_specs=SMEM,
        name="plan",
    )(lengths, to_group, to_slot)


def reached(group, seq, k, sign):
    sign = sign * (1 - 2 * (group % 2))
    chips = SEQ // CORES
    chip = (seq // CORES + sign * (k // CORES) + chips) % chips
    return chip * CORES + (seq + k) % CORES


def block_columns(k, device_width, chunk):
    other = reached(lax.axis_index("dp"), lax.axis_index("seq"), k, 1)
    start = pl.multiple_of(other * device_width + chunk[0] * HEAD, HEAD)
    return pl.ds(start, chunk[1] * HEAD)


def pack_kernel(chunk, qkv, cotangent, *refs):
    outs, (held, come, go) = refs[:SEQ], refs[SEQ:]
    device_width = qkv.shape[-1] // SEQ
    arrive = []
    for k in range(SEQ):
        columns = block_columns(k, device_width, chunk)
        arrive.append(
            (
                pltpu.make_async_copy(
                    qkv.at[:, 0, :, :, columns], held.at[k, pl.ds(0, 3)], come.at[k, 0]
                ),
                pltpu.make_async_copy(
                    cotangent.at[0, :, :, columns], held.at[k, 3], come.at[k, 1]
                ),
            )
        )
    leave = [pltpu.make_async_copy(held.at[k], outs[k], go.at[k]) for k in range(SEQ)]
    for pair in arrive:
        for copy in pair:
            copy.start()
    for pair, copy in zip(arrive, leave):
        for part in pair:
            part.wait()
        copy.start()
    for copy in leave:
        copy.wait()


def pack(qkv, cotangent, chunk):
    _, slots, rows, _ = cotangent.shape
    shape = (ARRAYS, slots, rows, chunk[1] * HEAD)
    return pl.pallas_call(
        functools.partial(pack_kernel, chunk),
        out_shape=[jax.ShapeDtypeStruct(shape, qkv.dtype)] * SEQ,
        in_specs=[ANY, ANY],
        out_specs=[ANY] * SEQ,
        scratch_shapes=[
            pltpu.VMEM((SEQ, *shape), qkv.dtype),
            pltpu.SemaphoreType.DMA((SEQ, 2)),
            pltpu.SemaphoreType.DMA((SEQ,)),
        ],
        name="pack",
    )(qkv, cotangent)


def exchange(parts, sign):
    received = list(parts)
    for k in ORDER:
        pairs = [
            (group * SEQ + i, group * SEQ + reached(group, i, k, sign))
            for group in range(lax.axis_size("dp"))
            for i in range(SEQ)
        ]
        received[k] = lax.ppermute(parts[k], ("dp", "seq"), pairs)
    return received


def place_blocks():
    group, seq = lax.axis_index("dp"), lax.axis_index("seq")
    return [reached(group, seq, k, -1) for k in range(SEQ)]


def block_rows(rows):
    return [pl.ds(pl.multiple_of(block * rows, rows), rows) for block in place_blocks()]


def token_numbers(shape, axis):
    rows = shape[axis] // SEQ
    piece = shape[:axis] + (rows,) + shape[axis + 1 :]
    within = lax.broadcasted_iota(jnp.int32, piece, axis)
    return jnp.concatenate([within + block * rows for block in place_blocks()], axis=axis)


def head_columns(head):
    return slice(head * HEAD, (head + 1) * HEAD)


def gathered(parts, array, slot, columns):
    return jnp.concatenate([part[array, slot, :, columns] for part in parts], axis=0)


def dot(a, b, a_axis, b_axis):
    return lax.dot_general(
        a, b, (((a_axis,), (b_axis,)), ((), ())), preferred_element_type=jnp.float32
    )


def scores_of(queries, keys, key_mask):
    return dot(keys, queries, 1, 1) * (HEAD**-0.5 * LOG2E) + key_mask


def mask_of_keys(tokens, count):
    return jnp.where(token_numbers((tokens, 1), 0) < count, 0.0, NEGATIVE)


def forward_kernel(plan, *refs):
    parts, (out, stats, *gifts) = refs[:SEQ], refs[SEQ:]
    slots, tokens, width = out.shape
    rows = tokens // SEQ
    heads = width // HEAD
    for slot in range(slots):
        count = plan[8 + slot]

        @pl.when(count == 0)
        def _():
            out[slot] = jnp.zeros_like(out[slot])

        @pl.when(count > 0)
        def _():
            key_mask = mask_of_keys(tokens, count)
            valid_queries = token_numbers((tokens, HEAD), 0) < count
            for head in range(heads):
                columns = head_columns(head)
                queries, keys, values = (gathered(parts, n, slot, columns) for n in range(3))
                scores = scores_of(queries, keys, key_mask)
                largest = jnp.max(scores, axis=0, keepdims=True)
                exponent = jnp.exp2(scores - largest)
                total = jnp.sum(exponent, axis=0, keepdims=True)
                weights = (exponent * (1.0 / total)).astype(jnp.bfloat16)
                output = dot(values, weights, 0, 0).T
                output = jnp.where(valid_queries, output, 0.0).astype(jnp.bfloat16)
                out[slot, :, columns] = output
                stats[slot, head : head + 1, :] = largest + jnp.log2(total)

    for number, gift in enumerate(gifts):
        for slot in range(slots):
            chosen = plan[2 * number + 1] == slot

            @pl.when((plan[2 * number] == 1) & chosen)
            def _():
                for k, held in enumerate(block_rows(rows)):
                    gift[held] = out[slot, k * rows : (k + 1) * rows]

            @pl.when((plan[2 * number] == 2) & chosen)
            def _():
                for held, part in zip(block_rows(rows), parts):
                    gift[held] = part[3, slot]


def forward(plan, parts):
    _, slots, rows, width = parts[0].shape
    tokens = rows * SEQ
    gift = jax.ShapeDtypeStruct((tokens, width), jnp.bfloat16)
    return pl.pallas_call(
        forward_kernel,
        out_shape=[
            jax.ShapeDtypeStruct((slots, tokens, width), jnp.bfloat16),
            jax.ShapeDtypeStruct((slots, 8, tokens), jnp.float32),
            gift,
            gift,
        ],
        in_specs=[SMEM] + [VMEM] * SEQ,
        out_specs=[VMEM] * 4,
        compiler_params=pltpu.CompilerParams(vmem_limit_bytes=40 << 20),
        name="forward",
    )(plan, *parts)


def backward_kernel(plan, *refs):
    parts, (home_out, stats, even, odd), outs = refs[:SEQ], refs[SEQ : SEQ + 4], refs[SEQ + 4 :]
    slots, tokens, width = home_out.shape
    rows = tokens // SEQ
    heads = width // HEAD
    for slot in range(slots):
        count = plan[8 + slot]

        @pl.when(plan[6 + slot] == 0)
        def _():
            for k, out in enumerate(outs):
                out[0, slot] = home_out[slot, k * rows : (k + 1) * rows]

        for choice, source in ((1, even), (2, odd)):

            @pl.when(plan[6 + slot] == choice)
            def _():
                for held, out in zip(block_rows(rows), outs):
                    out[0, slot] = source[held]

        @pl.when(plan[6 + slot] == 3)
        def _():
            for out in outs:
                out[0, slot] = jnp.zeros_like(out[0, slot])

        @pl.when(count == 0)
        def _():
            for out in outs:
                for array in range(1, ARRAYS):
                    out[array, slot] = jnp.zeros_like(out[array, slot])

        @pl.when(count > 0)
        def _():
            source = plan[4 + slot]
            key_mask = mask_of_keys(tokens, count)
            valid_queries = token_numbers((tokens, HEAD), 0) < count
            factor = HEAD**-0.5
            for head in range(heads):
                columns = head_columns(head)
                queries, keys, values, own = (
                    gathered(parts, n, slot, columns) for n in range(ARRAYS)
                )
                moved = [
                    jnp.where(source == 1, even[held, columns], odd[held, columns])
                    for held in block_rows(rows)
                ]
                moved = jnp.concatenate(moved, axis=0)
                upstream = jnp.where(source == 0, own, moved)
                upstream = jnp.where(valid_queries, upstream, jnp.zeros_like(upstream))
                scores = scores_of(queries, keys, key_mask)
                weights = jnp.exp2(scores - stats[slot, head : head + 1, :])
                grad_values = dot(weights.astype(jnp.bfloat16), upstream, 1, 0)
                grad_weights = dot(values, upstream, 1, 1)
                inner = jnp.sum(grad_weights * weights, axis=0, keepdims=True)
                score_grad = (weights * (grad_weights - inner)).astype(jnp.bfloat16)
                grad_queries = dot(keys, score_grad, 0, 0).T * factor
                grad_keys = dot(score_grad, queries, 1, 0) * factor
                for n, grad in enumerate((grad_queries, grad_keys, grad_values)):
                    grad = grad.astype(jnp.bfloat16)
                    for k, out in enumerate(outs):
                        out[1 + n, slot, :, columns] = grad[k * rows : (k + 1) * rows]


def backward(plan, parts, home_out, stats, even, odd):
    return pl.pallas_call(
        backward_kernel,
        out_shape=[jax.ShapeDtypeStruct(parts[0].shape, jnp.bfloat16)] * SEQ,
        in_specs=[SMEM] + [VMEM] * (SEQ + 4),
        out_specs=[VMEM] * SEQ,
        compiler_params=pltpu.CompilerParams(vmem_limit_bytes=48 << 20),
        name="backward",
    )(plan, *parts, home_out, stats, even, odd)


def unpack_kernel(chunk, steps, *refs):
    parts, (attended, grads, sem) = refs[: len(steps)], refs[-3:]
    device_width = grads.shape[-1] // SEQ
    copies = []
    for k, part in zip(steps, parts):
        columns = block_columns(k, device_width, chunk)
        copies += [
            pltpu.make_async_copy(part.at[0], attended.at[0, :, :, columns], sem.at[k, 0]),
            pltpu.make_async_copy(
                part.at[pl.ds(1, 3)], grads.at[:, 0, :, :, columns], sem.at[k, 1]
            ),
        ]
    for copy in copies:
        copy.start()
    for copy in copies:
        copy.wait()


def unpack(parts, steps, chunk, device_heads, filled=()):
    parts = [parts[k] for k in steps]
    _, slots, rows, _ = parts[0].shape
    features = device_heads * HEAD * SEQ
    return pl.pallas_call(
        functools.partial(unpack_kernel, chunk, steps),
        out_shape=[
            jax.ShapeDtypeStruct((1, slots, rows, features), jnp.bfloat16),
            jax.ShapeDtypeStruct((3, 1, slots, rows, features), jnp.bfloat16),
        ],
        in_specs=[VMEM] * len(steps) + [ANY] * len(filled),
        out_specs=[ANY, ANY],
        input_output_aliases={len(steps) + n: n for n in range(len(filled))},
        scratch_shapes=[pltpu.SemaphoreType.DMA((SEQ, 2))],
        name="unpack",
    )(*parts, *filled)


def swap(kind, gift, first, groups):
    pairs = []
    for low in range(first, groups - 1, 2):
        pairs += [(low, low + 1), (low + 1, low)]
    return lax.cond(
        kind > 0, lambda gift: lax.ppermute(gift, "dp", pairs), lambda gift: gift, gift
    )


def after(value, *others):
    return lax.optimization_barrier((value, *others))[0]


def on_device(qkv, cotangent, lengths, to_group, to_slot):
    groups = lengths.shape[0]
    device_heads = qkv.shape[-1] // (HEAD * SEQ)
    plan = make_plan(lengths, to_group, to_slot)
    packed = [pack(qkv, cotangent, chunk) for chunk in CHUNKS]
    arrived = [exchange(parts, 1) for parts in packed]
    returned = []
    for parts in arrived:
        home_out, stats, *gifts = forward(plan, parts)
        even, odd = (swap(plan[2 * n], gifts[n], n, groups) for n in range(2))
        returned.append(exchange(backward(plan, parts, home_out, stats, even, odd), -1))
    results = ()
    for parts, chunk in zip(returned, CHUNKS):
        for steps in ((0, *ORDER[:4]), ORDER[4:]):
            results = unpack(parts, steps, chunk, device_heads, results)
    return tuple(results)


def solution(mesh):
    in_specs = (P(None, "dp", None, "seq", None), P("dp", None, "seq", None), P(), P(), P())
    out_specs = (P("dp", None, "seq", None), P(None, "dp", None, "seq", None))
    return jax.shard_map(
        on_device, mesh=mesh, in_specs=in_specs, out_specs=out_specs, check_vma=False
    )
```

```python
import functools

import jax
import jax.numpy as jnp
from jax import lax
from jax.experimental import pallas as pl
from jax.experimental.pallas import tpu as pltpu
from jax.sharding import PartitionSpec as P

HEAD = 128
SEQ = 8
ARRAYS = 4
NEGATIVE = -1e30
LOG2E = 1.4426950408889634
CORES = 2
ORDER = (4, 6, 5, 7, 1, 2, 3)
CHUNKS = ((0, 3),)
ANY = pl.BlockSpec(memory_space=pl.ANY)
VMEM = pl.BlockSpec(memory_space=pltpu.VMEM)
SMEM = pl.BlockSpec(memory_space=pltpu.SMEM)


def partners(group):
    odd = lax.rem(group, 2)
    return group + 1 - 2 * odd, group - 1 + 2 * odd


def plan_kernel(lengths, to_group, to_slot, plan):
    groups = lengths.shape[0]
    me = lax.axis_index("dp")
    grad_source = [jnp.int32(0), jnp.int32(0)]
    out_source = []
    for slot in range(2):
        stays = (lengths[me, slot] > 0) & (to_group[me, slot] == me)
        out_source.append(jnp.where(stays, 0, 3))
    for number, other in enumerate(partners(me)):
        inside = (other >= 0) & (other < groups)
        there = jnp.clip(other, 0, groups - 1)
        kind = jnp.int32(0)
        given = jnp.int32(0)
        for slot in range(2):
            leaves = inside & (lengths[me, slot] > 0) & (to_group[me, slot] == other)
            arrives = inside & (lengths[there, slot] > 0) & (to_group[there, slot] == me)
            lands = to_slot[there, slot]
            kind = jnp.where(leaves, 1, jnp.where(arrives, 2, kind))
            given = jnp.where(leaves, slot, jnp.where(arrives, lands, given))
            grad_source[slot] = jnp.where(leaves, number + 1, grad_source[slot])
            for here in range(2):
                out_source[here] = jnp.where(arrives & (lands == here), number + 1, out_source[here])
        plan[2 * number] = kind
        plan[2 * number + 1] = given
    for slot in range(2):
        plan[4 + slot] = grad_source[slot]
        plan[6 + slot] = out_source[slot]
        plan[8 + slot] = lengths[me, slot]


def make_plan(lengths, to_group, to_slot):
    return pl.pallas_call(
        plan_kernel,
        out_shape=jax.ShapeDtypeStruct((10,), jnp.int32),
        in_specs=[SMEM] * 3,
        out_specs=SMEM,
        name="plan",
    )(lengths, to_group, to_slot)


def reached(group, seq, k, sign):
    sign = sign * (1 - 2 * (group % 2))
    chips = SEQ // CORES
    chip = (seq // CORES + sign * (k // CORES) + chips) % chips
    return chip * CORES + (seq + k) % CORES


def block_columns(k, device_width, chunk):
    other = reached(lax.axis_index("dp"), lax.axis_index("seq"), k, 1)
    start = pl.multiple_of(other * device_width + chunk[0] * HEAD, HEAD)
    return pl.ds(start, chunk[1] * HEAD)


def pack_kernel(chunk, qkv, cotangent, *refs):
    outs, (held, come, go) = refs[:SEQ], refs[SEQ:]
    device_width = qkv.shape[-1] // SEQ
    arrive = []
    for k in range(SEQ):
        columns = block_columns(k, device_width, chunk)
        arrive.append(
            (
                pltpu.make_async_copy(
                    qkv.at[:, 0, :, :, columns], held.at[k, pl.ds(0, 3)], come.at[k, 0]
                ),
                pltpu.make_async_copy(
                    cotangent.at[0, :, :, columns], held.at[k, 3], come.at[k, 1]
                ),
            )
        )
    leave = [pltpu.make_async_copy(held.at[k], outs[k], go.at[k]) for k in range(SEQ)]
    for pair in arrive:
        for copy in pair:
            copy.start()
    for pair, copy in zip(arrive, leave):
        for part in pair:
            part.wait()
        copy.start()
    for copy in leave:
        copy.wait()


def pack(qkv, cotangent, chunk):
    _, slots, rows, _ = cotangent.shape
    shape = (ARRAYS, slots, rows, chunk[1] * HEAD)
    return pl.pallas_call(
        functools.partial(pack_kernel, chunk),
        out_shape=[jax.ShapeDtypeStruct(shape, qkv.dtype)] * SEQ,
        in_specs=[ANY, ANY],
        out_specs=[ANY] * SEQ,
        scratch_shapes=[
            pltpu.VMEM((SEQ, *shape), qkv.dtype),
            pltpu.SemaphoreType.DMA((SEQ, 2)),
            pltpu.SemaphoreType.DMA((SEQ,)),
        ],
        name="pack",
    )(qkv, cotangent)


def exchange(parts, sign):
    received = list(parts)
    for k in ORDER:
        pairs = [
            (group * SEQ + i, group * SEQ + reached(group, i, k, sign))
            for group in range(lax.axis_size("dp"))
            for i in range(SEQ)
        ]
        received[k] = lax.ppermute(parts[k], ("dp", "seq"), pairs)
    return received


def place_blocks():
    group, seq = lax.axis_index("dp"), lax.axis_index("seq")
    return [reached(group, seq, k, -1) for k in range(SEQ)]


def block_rows(rows):
    return [pl.ds(pl.multiple_of(block * rows, rows), rows) for block in place_blocks()]


def token_numbers(shape, axis):
    rows = shape[axis] // SEQ
    piece = shape[:axis] + (rows,) + shape[axis + 1 :]
    within = lax.broadcasted_iota(jnp.int32, piece, axis)
    return jnp.concatenate([within + block * rows for block in place_blocks()], axis=axis)


def head_columns(head):
    return slice(head * HEAD, (head + 1) * HEAD)


def gathered(parts, array, slot, columns):
    return jnp.concatenate([part[array, slot, :, columns] for part in parts], axis=0)


def dot(a, b, a_axis, b_axis):
    return lax.dot_general(
        a, b, (((a_axis,), (b_axis,)), ((), ())), preferred_element_type=jnp.float32
    )


def scores_of(queries, keys, key_mask):
    return dot(keys, queries, 1, 1) * (HEAD**-0.5 * LOG2E) + key_mask


def mask_of_keys(tokens, count):
    return jnp.where(token_numbers((tokens, 1), 0) < count, 0.0, NEGATIVE)


def forward_kernel(plan, *refs):
    parts, (out, stats, *gifts) = refs[:SEQ], refs[SEQ:]
    slots, tokens, width = out.shape
    rows = tokens // SEQ
    heads = width // HEAD
    for slot in range(slots):
        count = plan[8 + slot]

        @pl.when(count == 0)
        def _():
            out[slot] = jnp.zeros_like(out[slot])

        @pl.when(count > 0)
        def _():
            key_mask = mask_of_keys(tokens, count)
            valid_queries = token_numbers((tokens, HEAD), 0) < count
            for head in range(heads):
                columns = head_columns(head)
                queries, keys, values = (gathered(parts, n, slot, columns) for n in range(3))
                scores = scores_of(queries, keys, key_mask)
                largest = jnp.max(scores, axis=0, keepdims=True)
                exponent = jnp.exp2(scores - largest)
                total = jnp.sum(exponent, axis=0, keepdims=True)
                weights = (exponent * (1.0 / total)).astype(jnp.bfloat16)
                output = dot(values, weights, 0, 0).T
                output = jnp.where(valid_queries, output, 0.0).astype(jnp.bfloat16)
                out[slot, :, columns] = output
                stats[slot, head : head + 1, :] = largest + jnp.log2(total)

    for number, gift in enumerate(gifts):
        for slot in range(slots):
            chosen = plan[2 * number + 1] == slot

            @pl.when((plan[2 * number] == 1) & chosen)
            def _():
                for k, held in enumerate(block_rows(rows)):
                    gift[held] = out[slot, k * rows : (k + 1) * rows]

            @pl.when((plan[2 * number] == 2) & chosen)
            def _():
                for held, part in zip(block_rows(rows), parts):
                    gift[held] = part[3, slot]


def forward(plan, parts):
    _, slots, rows, width = parts[0].shape
    tokens = rows * SEQ
    gift = jax.ShapeDtypeStruct((tokens, width), jnp.bfloat16)
    return pl.pallas_call(
        forward_kernel,
        out_shape=[
            jax.ShapeDtypeStruct((slots, tokens, width), jnp.bfloat16),
            jax.ShapeDtypeStruct((slots, 8, tokens), jnp.float32),
            gift,
            gift,
        ],
        in_specs=[SMEM] + [VMEM] * SEQ,
        out_specs=[VMEM] * 4,
        compiler_params=pltpu.CompilerParams(vmem_limit_bytes=40 << 20),
        name="forward",
    )(plan, *parts)


def backward_kernel(plan, *refs):
    parts, (home_out, stats, even, odd), outs = refs[:SEQ], refs[SEQ : SEQ + 4], refs[SEQ + 4 :]
    slots, tokens, width = home_out.shape
    rows = tokens // SEQ
    heads = width // HEAD
    for slot in range(slots):
        count = plan[8 + slot]

        @pl.when(plan[6 + slot] == 0)
        def _():
            for k, out in enumerate(outs):
                out[0, slot] = home_out[slot, k * rows : (k + 1) * rows]

        for choice, source in ((1, even), (2, odd)):

            @pl.when(plan[6 + slot] == choice)
            def _():
                for held, out in zip(block_rows(rows), outs):
                    out[0, slot] = source[held]

        @pl.when(plan[6 + slot] == 3)
        def _():
            for out in outs:
                out[0, slot] = jnp.zeros_like(out[0, slot])

        @pl.when(count == 0)
        def _():
            for out in outs:
                for array in range(1, ARRAYS):
                    out[array, slot] = jnp.zeros_like(out[array, slot])

        @pl.when(count > 0)
        def _():
            source = plan[4 + slot]
            key_mask = mask_of_keys(tokens, count)
            valid_queries = token_numbers((tokens, HEAD), 0) < count
            factor = HEAD**-0.5
            for head in range(heads):
                columns = head_columns(head)
                queries, keys, values, own = (
                    gathered(parts, n, slot, columns) for n in range(ARRAYS)
                )
                moved = [
                    jnp.where(source == 1, even[held, columns], odd[held, columns])
                    for held in block_rows(rows)
                ]
                moved = jnp.concatenate(moved, axis=0)
                upstream = jnp.where(source == 0, own, moved)
                upstream = jnp.where(valid_queries, upstream, jnp.zeros_like(upstream))
                scores = scores_of(queries, keys, key_mask)
                weights = jnp.exp2(scores - stats[slot, head : head + 1, :])
                grad_values = dot(weights.astype(jnp.bfloat16), upstream, 1, 0)
                grad_weights = dot(values, upstream, 1, 1)
                inner = jnp.sum(grad_weights * weights, axis=0, keepdims=True)
                score_grad = (weights * (grad_weights - inner)).astype(jnp.bfloat16)
                grad_queries = dot(keys, score_grad, 0, 0).T * factor
                grad_keys = dot(score_grad, queries, 1, 0) * factor
                for n, grad in enumerate((grad_queries, grad_keys, grad_values)):
                    grad = grad.astype(jnp.bfloat16)
                    for k, out in enumerate(outs):
                        out[1 + n, slot, :, columns] = grad[k * rows : (k + 1) * rows]


def backward(plan, parts, home_out, stats, even, odd):
    return pl.pallas_call(
        backward_kernel,
        out_shape=[jax.ShapeDtypeStruct(parts[0].shape, jnp.bfloat16)] * SEQ,
        in_specs=[SMEM] + [VMEM] * (SEQ + 4),
        out_specs=[VMEM] * SEQ,
        compiler_params=pltpu.CompilerParams(vmem_limit_bytes=48 << 20),
        name="backward",
    )(plan, *parts, home_out, stats, even, odd)


def unpack_kernel(chunk, steps, *refs):
    parts, (attended, grads, sem) = refs[: len(steps)], refs[-3:]
    device_width = grads.shape[-1] // SEQ
    copies = []
    for k, part in zip(steps, parts):
        columns = block_columns(k, device_width, chunk)
        copies += [
            pltpu.make_async_copy(part.at[0], attended.at[0, :, :, columns], sem.at[k, 0]),
            pltpu.make_async_copy(
                part.at[pl.ds(1, 3)], grads.at[:, 0, :, :, columns], sem.at[k, 1]
            ),
        ]
    for copy in copies:
        copy.start()
    for copy in copies:
        copy.wait()


def unpack(parts, steps, chunk, device_heads, filled=()):
    parts = [parts[k] for k in steps]
    _, slots, rows, _ = parts[0].shape
    features = device_heads * HEAD * SEQ
    return pl.pallas_call(
        functools.partial(unpack_kernel, chunk, steps),
        out_shape=[
            jax.ShapeDtypeStruct((1, slots, rows, features), jnp.bfloat16),
            jax.ShapeDtypeStruct((3, 1, slots, rows, features), jnp.bfloat16),
        ],
        in_specs=[VMEM] * len(steps) + [ANY] * len(filled),
        out_specs=[ANY, ANY],
        input_output_aliases={len(steps) + n: n for n in range(len(filled))},
        scratch_shapes=[pltpu.SemaphoreType.DMA((SEQ, 2))],
        name="unpack",
    )(*parts, *filled)


def swap(kind, gift, first, groups):
    pairs = []
    for low in range(first, groups - 1, 2):
        pairs += [(low, low + 1), (low + 1, low)]
    return lax.cond(
        kind > 0, lambda gift: lax.ppermute(gift, "dp", pairs), lambda gift: gift, gift
    )


def after(value, *others):
    return lax.optimization_barrier((value, *others))[0]


def on_device(qkv, cotangent, lengths, to_group, to_slot):
    groups = lengths.shape[0]
    device_heads = qkv.shape[-1] // (HEAD * SEQ)
    plan = make_plan(lengths, to_group, to_slot)
    packed = [pack(qkv, cotangent, chunk) for chunk in CHUNKS]
    arrived = [exchange(parts, 1) for parts in packed]
    returned = []
    for parts in arrived:
        home_out, stats, *gifts = forward(plan, parts)
        even, odd = (swap(plan[2 * n], gifts[n], n, groups) for n in range(2))
        returned.append(exchange(backward(plan, parts, home_out, stats, even, odd), -1))
    results = ()
    for parts, chunk in zip(returned, CHUNKS):
        for steps in ((0, *ORDER[:4]), ORDER[4:]):
            results = unpack(parts, steps, chunk, device_heads, results)
    return tuple(results)


def solution(mesh):
    in_specs = (P(None, "dp", None, "seq", None), P("dp", None, "seq", None), P(), P(), P())
    out_specs = (P("dp", None, "seq", None), P(None, "dp", None, "seq", None))
    return jax.shard_map(
        on_device, mesh=mesh, in_specs=in_specs, out_specs=out_specs, check_vma=False
    )
```

```python
import functools

import jax
import jax.numpy as jnp
from jax import lax
from jax.experimental import pallas as pl
from jax.experimental.pallas import tpu as pltpu
from jax.sharding import PartitionSpec as P

HEAD = 128
SEQ = 8
ARRAYS = 4
NEGATIVE = -1e30
LOG2E = 1.4426950408889634
CORES = 2
ORDER = (4, 6, 5, 7, 2, 1, 3)
CHUNKS = ((0, 3),)
ANY = pl.BlockSpec(memory_space=pl.ANY)
VMEM = pl.BlockSpec(memory_space=pltpu.VMEM)
SMEM = pl.BlockSpec(memory_space=pltpu.SMEM)


def partners(group):
    odd = lax.rem(group, 2)
    return group + 1 - 2 * odd, group - 1 + 2 * odd


def plan_kernel(lengths, to_group, to_slot, plan):
    groups = lengths.shape[0]
    me = lax.axis_index("dp")
    grad_source = [jnp.int32(0), jnp.int32(0)]
    out_source = []
    for slot in range(2):
        stays = (lengths[me, slot] > 0) & (to_group[me, slot] == me)
        out_source.append(jnp.where(stays, 0, 3))
    for number, other in enumerate(partners(me)):
        inside = (other >= 0) & (other < groups)
        there = jnp.clip(other, 0, groups - 1)
        kind = jnp.int32(0)
        given = jnp.int32(0)
        for slot in range(2):
            leaves = inside & (lengths[me, slot] > 0) & (to_group[me, slot] == other)
            arrives = inside & (lengths[there, slot] > 0) & (to_group[there, slot] == me)
            lands = to_slot[there, slot]
            kind = jnp.where(leaves, 1, jnp.where(arrives, 2, kind))
            given = jnp.where(leaves, slot, jnp.where(arrives, lands, given))
            grad_source[slot] = jnp.where(leaves, number + 1, grad_source[slot])
            for here in range(2):
                out_source[here] = jnp.where(arrives & (lands == here), number + 1, out_source[here])
        plan[2 * number] = kind
        plan[2 * number + 1] = given
    for slot in range(2):
        plan[4 + slot] = grad_source[slot]
        plan[6 + slot] = out_source[slot]
        plan[8 + slot] = lengths[me, slot]


def make_plan(lengths, to_group, to_slot):
    return pl.pallas_call(
        plan_kernel,
        out_shape=jax.ShapeDtypeStruct((10,), jnp.int32),
        in_specs=[SMEM] * 3,
        out_specs=SMEM,
        name="plan",
    )(lengths, to_group, to_slot)


def reached(group, seq, k, sign):
    sign = sign * (1 - 2 * (group % 2))
    chips = SEQ // CORES
    chip = (seq // CORES + sign * (k // CORES) + chips) % chips
    return chip * CORES + (seq + k) % CORES


def block_columns(k, device_width, chunk):
    other = reached(lax.axis_index("dp"), lax.axis_index("seq"), k, 1)
    start = pl.multiple_of(other * device_width + chunk[0] * HEAD, HEAD)
    return pl.ds(start, chunk[1] * HEAD)


def pack_kernel(chunk, qkv, cotangent, *refs):
    outs, (held, come, go) = refs[:SEQ], refs[SEQ:]
    device_width = qkv.shape[-1] // SEQ
    arrive = []
    for k in range(SEQ):
        columns = block_columns(k, device_width, chunk)
        arrive.append(
            (
                pltpu.make_async_copy(
                    qkv.at[:, 0, :, :, columns], held.at[k, pl.ds(0, 3)], come.at[k, 0]
                ),
                pltpu.make_async_copy(
                    cotangent.at[0, :, :, columns], held.at[k, 3], come.at[k, 1]
                ),
            )
        )
    leave = [pltpu.make_async_copy(held.at[k], outs[k], go.at[k]) for k in range(SEQ)]
    for pair in arrive:
        for copy in pair:
            copy.start()
    for pair, copy in zip(arrive, leave):
        for part in pair:
            part.wait()
        copy.start()
    for copy in leave:
        copy.wait()


def pack(qkv, cotangent, chunk):
    _, slots, rows, _ = cotangent.shape
    shape = (ARRAYS, slots, rows, chunk[1] * HEAD)
    return pl.pallas_call(
        functools.partial(pack_kernel, chunk),
        out_shape=[jax.ShapeDtypeStruct(shape, qkv.dtype)] * SEQ,
        in_specs=[ANY, ANY],
        out_specs=[ANY] * SEQ,
        scratch_shapes=[
            pltpu.VMEM((SEQ, *shape), qkv.dtype),
            pltpu.SemaphoreType.DMA((SEQ, 2)),
            pltpu.SemaphoreType.DMA((SEQ,)),
        ],
        name="pack",
    )(qkv, cotangent)


def exchange(parts, sign):
    received = list(parts)
    for k in ORDER:
        pairs = [
            (group * SEQ + i, group * SEQ + reached(group, i, k, sign))
            for group in range(lax.axis_size("dp"))
            for i in range(SEQ)
        ]
        received[k] = lax.ppermute(parts[k], ("dp", "seq"), pairs)
    return received


def place_blocks():
    group, seq = lax.axis_index("dp"), lax.axis_index("seq")
    return [reached(group, seq, k, -1) for k in range(SEQ)]


def block_rows(rows):
    return [pl.ds(pl.multiple_of(block * rows, rows), rows) for block in place_blocks()]


def token_numbers(shape, axis):
    rows = shape[axis] // SEQ
    piece = shape[:axis] + (rows,) + shape[axis + 1 :]
    within = lax.broadcasted_iota(jnp.int32, piece, axis)
    return jnp.concatenate([within + block * rows for block in place_blocks()], axis=axis)


def head_columns(head):
    return slice(head * HEAD, (head + 1) * HEAD)


def gathered(parts, array, slot, columns):
    return jnp.concatenate([part[array, slot, :, columns] for part in parts], axis=0)


def dot(a, b, a_axis, b_axis):
    return lax.dot_general(
        a, b, (((a_axis,), (b_axis,)), ((), ())), preferred_element_type=jnp.float32
    )


def scores_of(queries, keys, key_mask):
    return dot(keys, queries, 1, 1) * (HEAD**-0.5 * LOG2E) + key_mask


def mask_of_keys(tokens, count):
    return jnp.where(token_numbers((tokens, 1), 0) < count, 0.0, NEGATIVE)


def forward_kernel(plan, *refs):
    parts, (out, stats, *gifts) = refs[:SEQ], refs[SEQ:]
    slots, tokens, width = out.shape
    rows = tokens // SEQ
    heads = width // HEAD
    for slot in range(slots):
        count = plan[8 + slot]

        @pl.when(count == 0)
        def _():
            out[slot] = jnp.zeros_like(out[slot])

        @pl.when(count > 0)
        def _():
            key_mask = mask_of_keys(tokens, count)
            valid_queries = token_numbers((tokens, HEAD), 0) < count
            for head in range(heads):
                columns = head_columns(head)
                queries, keys, values = (gathered(parts, n, slot, columns) for n in range(3))
                scores = scores_of(queries, keys, key_mask)
                largest = jnp.max(scores, axis=0, keepdims=True)
                exponent = jnp.exp2(scores - largest)
                total = jnp.sum(exponent, axis=0, keepdims=True)
                weights = (exponent * (1.0 / total)).astype(jnp.bfloat16)
                output = dot(values, weights, 0, 0).T
                output = jnp.where(valid_queries, output, 0.0).astype(jnp.bfloat16)
                out[slot, :, columns] = output
                stats[slot, head : head + 1, :] = largest + jnp.log2(total)

    for number, gift in enumerate(gifts):
        for slot in range(slots):
            chosen = plan[2 * number + 1] == slot

            @pl.when((plan[2 * number] == 1) & chosen)
            def _():
                for k, held in enumerate(block_rows(rows)):
                    gift[held] = out[slot, k * rows : (k + 1) * rows]

            @pl.when((plan[2 * number] == 2) & chosen)
            def _():
                for held, part in zip(block_rows(rows), parts):
                    gift[held] = part[3, slot]


def forward(plan, parts):
    _, slots, rows, width = parts[0].shape
    tokens = rows * SEQ
    gift = jax.ShapeDtypeStruct((tokens, width), jnp.bfloat16)
    return pl.pallas_call(
        forward_kernel,
        out_shape=[
            jax.ShapeDtypeStruct((slots, tokens, width), jnp.bfloat16),
            jax.ShapeDtypeStruct((slots, 8, tokens), jnp.float32),
            gift,
            gift,
        ],
        in_specs=[SMEM] + [VMEM] * SEQ,
        out_specs=[VMEM] * 4,
        compiler_params=pltpu.CompilerParams(vmem_limit_bytes=40 << 20),
        name="forward",
    )(plan, *parts)


def backward_kernel(plan, *refs):
    parts, (home_out, stats, even, odd), outs = refs[:SEQ], refs[SEQ : SEQ + 4], refs[SEQ + 4 :]
    slots, tokens, width = home_out.shape
    rows = tokens // SEQ
    heads = width // HEAD
    for slot in range(slots):
        count = plan[8 + slot]

        @pl.when(plan[6 + slot] == 0)
        def _():
            for k, out in enumerate(outs):
                out[0, slot] = home_out[slot, k * rows : (k + 1) * rows]

        for choice, source in ((1, even), (2, odd)):

            @pl.when(plan[6 + slot] == choice)
            def _():
                for held, out in zip(block_rows(rows), outs):
                    out[0, slot] = source[held]

        @pl.when(plan[6 + slot] == 3)
        def _():
            for out in outs:
                out[0, slot] = jnp.zeros_like(out[0, slot])

        @pl.when(count == 0)
        def _():
            for out in outs:
                for array in range(1, ARRAYS):
                    out[array, slot] = jnp.zeros_like(out[array, slot])

        @pl.when(count > 0)
        def _():
            source = plan[4 + slot]
            key_mask = mask_of_keys(tokens, count)
            valid_queries = token_numbers((tokens, HEAD), 0) < count
            factor = HEAD**-0.5
            for head in range(heads):
                columns = head_columns(head)
                queries, keys, values, own = (
                    gathered(parts, n, slot, columns) for n in range(ARRAYS)
                )
                moved = [
                    jnp.where(source == 1, even[held, columns], odd[held, columns])
                    for held in block_rows(rows)
                ]
                moved = jnp.concatenate(moved, axis=0)
                upstream = jnp.where(source == 0, own, moved)
                upstream = jnp.where(valid_queries, upstream, jnp.zeros_like(upstream))
                scores = scores_of(queries, keys, key_mask)
                weights = jnp.exp2(scores - stats[slot, head : head + 1, :])
                grad_values = dot(weights.astype(jnp.bfloat16), upstream, 1, 0)
                grad_weights = dot(values, upstream, 1, 1)
                inner = jnp.sum(grad_weights * weights, axis=0, keepdims=True)
                score_grad = (weights * (grad_weights - inner)).astype(jnp.bfloat16)
                grad_queries = dot(keys, score_grad, 0, 0).T * factor
                grad_keys = dot(score_grad, queries, 1, 0) * factor
                for n, grad in enumerate((grad_queries, grad_keys, grad_values)):
                    grad = grad.astype(jnp.bfloat16)
                    for k, out in enumerate(outs):
                        out[1 + n, slot, :, columns] = grad[k * rows : (k + 1) * rows]


def backward(plan, parts, home_out, stats, even, odd):
    return pl.pallas_call(
        backward_kernel,
        out_shape=[jax.ShapeDtypeStruct(parts[0].shape, jnp.bfloat16)] * SEQ,
        in_specs=[SMEM] + [VMEM] * (SEQ + 4),
        out_specs=[VMEM] * SEQ,
        compiler_params=pltpu.CompilerParams(vmem_limit_bytes=48 << 20),
        name="backward",
    )(plan, *parts, home_out, stats, even, odd)


def unpack_kernel(chunk, steps, *refs):
    parts, (attended, grads, sem) = refs[: len(steps)], refs[-3:]
    device_width = grads.shape[-1] // SEQ
    copies = []
    for k, part in zip(steps, parts):
        columns = block_columns(k, device_width, chunk)
        copies += [
            pltpu.make_async_copy(part.at[0], attended.at[0, :, :, columns], sem.at[k, 0]),
            pltpu.make_async_copy(
                part.at[pl.ds(1, 3)], grads.at[:, 0, :, :, columns], sem.at[k, 1]
            ),
        ]
    for copy in copies:
        copy.start()
    for copy in copies:
        copy.wait()


def unpack(parts, steps, chunk, device_heads, filled=()):
    parts = [parts[k] for k in steps]
    _, slots, rows, _ = parts[0].shape
    features = device_heads * HEAD * SEQ
    return pl.pallas_call(
        functools.partial(unpack_kernel, chunk, steps),
        out_shape=[
            jax.ShapeDtypeStruct((1, slots, rows, features), jnp.bfloat16),
            jax.ShapeDtypeStruct((3, 1, slots, rows, features), jnp.bfloat16),
        ],
        in_specs=[VMEM] * len(steps) + [ANY] * len(filled),
        out_specs=[ANY, ANY],
        input_output_aliases={len(steps) + n: n for n in range(len(filled))},
        scratch_shapes=[pltpu.SemaphoreType.DMA((SEQ, 2))],
        name="unpack",
    )(*parts, *filled)


def swap(kind, gift, first, groups):
    pairs = []
    for low in range(first, groups - 1, 2):
        pairs += [(low, low + 1), (low + 1, low)]
    return lax.cond(
        kind > 0, lambda gift: lax.ppermute(gift, "dp", pairs), lambda gift: gift, gift
    )


def after(value, *others):
    return lax.optimization_barrier((value, *others))[0]


def on_device(qkv, cotangent, lengths, to_group, to_slot):
    groups = lengths.shape[0]
    device_heads = qkv.shape[-1] // (HEAD * SEQ)
    plan = make_plan(lengths, to_group, to_slot)
    packed = [pack(qkv, cotangent, chunk) for chunk in CHUNKS]
    arrived = [exchange(parts, 1) for parts in packed]
    returned = []
    for parts in arrived:
        home_out, stats, *gifts = forward(plan, parts)
        even, odd = (swap(plan[2 * n], gifts[n], n, groups) for n in range(2))
        returned.append(exchange(backward(plan, parts, home_out, stats, even, odd), -1))
    results = ()
    for parts, chunk in zip(returned, CHUNKS):
        for steps in ((0, *ORDER[:4]), ORDER[4:]):
            results = unpack(parts, steps, chunk, device_heads, results)
    return tuple(results)


def solution(mesh):
    in_specs = (P(None, "dp", None, "seq", None), P("dp", None, "seq", None), P(), P(), P())
    out_specs = (P("dp", None, "seq", None), P(None, "dp", None, "seq", None))
    return jax.shard_map(
        on_device, mesh=mesh, in_specs=in_specs, out_specs=out_specs, check_vma=False
    )
```
